32 devices in a mesh: pipe: 2 (over x), seq: 4 (over y, core), chan: 4 (over z).
Axes of the slice: x: 2, y: 2, z: 4, core: 2. Of those that a mesh axis runs over, the one named last changes fastest.
Arguments:
- fwd_in: bfloat16 [2, 512, 8192], P('pipe', 'seq', 'chan'), may hold values from -14 to 14
- saved_in: bfloat16 [2, 512, 8192], P('pipe', 'seq', 'chan'), may hold values from -14 to 14
- saved_conv: bfloat16 [2, 512, 8192], P('pipe', 'seq', 'chan'), may hold values from -5 to 5
- grad_out: bfloat16 [2, 512, 8192], P('pipe', 'seq', 'chan'), may hold values from -14 to 14
- filters: bfloat16 [2, 512, 8192], P('pipe', None, 'chan'), may hold values from -1.2 to 1.2
- mix_params: float32 [2, 7, 8192], P('pipe', None, 'chan'), may hold values from -1.5 to 1.5
- span_order: int32 [4], replicated, may hold values from 0 to 3, each once
Outputs:
- layer_out: bfloat16 [2, 512, 8192], P('pipe', 'seq', 'chan')
- input_grad: bfloat16 [2, 512, 8192], P('pipe', 'seq', 'chan')
- param_grad: float32 [2, 7, 8192], P('pipe', None, 'chan')
- received: bfloat16 [2, 512, 8192], P('pipe', 'seq', 'chan')
The draws below stay inside these ranges and needn't reach their ends.
Inputs may be any that keep to these rules, and one draw needn't show every extreme that they name: span_order holds each block position once.
All inputs are finite; a program needn't handle non-finite values.
Results may differ from the reference program's by a relative error of at most 0.015.
Values may be sent and summed in bfloat16 or wider, within the bound.
A program may use at most 192 MiB of HBM per device.

```python
import math
import jax
import jax.numpy as jnp
from jax import lax

D = 8192
TOK_DEV = 128
SEQ_LEN = 512
SPANS = 4
SEGMENTS = 2
N_SEQ = 4


def activation_law(key, rows_rise):
    key_base, key_cols = jax.random.split(key, 2)
    shape = (SEGMENTS, SEQ_LEN, D)
    base = jnp.clip(jax.random.normal(key_base, shape, jnp.float32), -4.0, 4.0)
    spread = jax.random.uniform(key_cols, (SEGMENTS, 1, D), jnp.float32, math.log(0.5), math.log(1.5))
    column_pos = jnp.arange(D, dtype=jnp.float32) / max(D - 1, 1)
    column_scale = jnp.exp(spread) * jnp.power(3.0, column_pos)[None, None, :] / 2.0
    row_pos = jnp.arange(SEQ_LEN, dtype=jnp.float32) / max(SEQ_LEN - 1, 1)
    row_scale = jnp.power(3.0, rows_rise * row_pos)[None, :, None] / (1.0 + rows_rise)
    return base * column_scale * row_scale


def draw_fwd_in(key, part):
    return activation_law(jax.random.fold_in(key, 11), 0.0).astype(jnp.bfloat16)


def draw_saved_in(key, part):
    return activation_law(jax.random.fold_in(key, 12), 0.0).astype(jnp.bfloat16)


def draw_grad_out(key, part):
    return activation_law(jax.random.fold_in(key, 13), 1.0).astype(jnp.bfloat16)


def draw_filters(key, part):
    key_rate, key_noise = jax.random.split(jax.random.fold_in(key, 21), 2)
    decay_rate = jnp.exp(jax.random.uniform(key_rate, (SEGMENTS, 1, D), jnp.float32, math.log(0.05 / SEQ_LEN), math.log(1.0 / 30.0)))
    lag_pos = jnp.arange(SEQ_LEN, dtype=jnp.float32)[None, :, None]
    amplitude = jnp.sqrt(2.0 * jnp.maximum(decay_rate, 1.0 / SEQ_LEN))
    noise = jnp.clip(jax.random.normal(key_noise, (SEGMENTS, SEQ_LEN, D), jnp.float32), -4.0, 4.0)
    taps = noise * jnp.exp(-decay_rate * lag_pos) * amplitude
    return jnp.clip(taps, -1.2, 1.2).astype(jnp.bfloat16)


def draw_mix_params(key, part):
    key_gain, key_mag, key_sign, key_bias = jax.random.split(jax.random.fold_in(key, 31), 4)
    gains = jax.random.uniform(key_gain, (SEGMENTS, 1, D), jnp.float32, 0.5, 1.5)
    magnitude = jax.random.uniform(key_mag, (SEGMENTS, 3, D), jnp.float32, 0.5, 1.5)
    biases = jnp.clip(0.5 * jax.random.normal(key_bias, (SEGMENTS, 3, D), jnp.float32), -1.5, 1.5)
    scales = magnitude * jnp.sign(jax.random.normal(key_sign, (SEGMENTS, 3, D), jnp.float32))
    rows = [gains[:, 0], scales[:, 0], biases[:, 0], scales[:, 1], biases[:, 1], scales[:, 2], biases[:, 2]]
    return jnp.stack(rows, axis=1)


def levels(stream_key, shape, cuts, smallest, largest):
    loudness, own = 1.0, jax.random.fold_in(stream_key, 6)
    for axis_at, blocks in cuts:
        steps = jnp.exp(jax.random.uniform(jax.random.fold_in(own, axis_at), (blocks,), jnp.float32, smallest / len(cuts), largest / len(cuts)))
        loudness = loudness * jnp.repeat(steps, shape[axis_at] // blocks).reshape([-1 if axis == axis_at else 1 for axis in range(len(shape))])
    return loudness


def bell_draw(stream_key, shape, deviation, most, cuts=(), kind=jnp.bfloat16):
    gain = levels(stream_key, shape, cuts, -0.22, 0.18) if cuts else 1.0
    drawn = jax.random.normal(stream_key, shape, jnp.float32) * deviation * gain
    return jnp.minimum(jnp.maximum(drawn, -most), most).astype(kind)


def setup_inputs(seed: int = 0) -> dict:
    key_of = jax.random.split(jax.random.key(seed), 8)
    fwd_in = draw_fwd_in(jax.random.fold_in(key_of[7], 71), 0)
    saved_in = draw_saved_in(jax.random.fold_in(key_of[7], 71), 0)
    saved_conv = bell_draw(key_of[2], (SEGMENTS, SEQ_LEN, D), 1.0, 5.0, ((0, 2), (1, 4), (2, 4)))
    grad_out = draw_grad_out(jax.random.fold_in(key_of[7], 71), 0)
    filters = draw_filters(jax.random.fold_in(key_of[7], 71), 0)
    mix_params = draw_mix_params(jax.random.fold_in(key_of[7], 71), 0)
    span_order = jax.random.permutation(key_of[6], N_SEQ).astype(jnp.int32)
    return {"fwd_in": fwd_in, "saved_in": saved_in, "saved_conv": saved_conv, "grad_out": grad_out, "filters": filters, "mix_params": mix_params, "span_order": span_order}


EPSILON = 1e-05

def mixer_fields(inputs, params):
    squares = lax.optimization_barrier(jnp.mean(inputs * inputs, axis=1, keepdims=True))
    inv_rms = lax.rsqrt(squares + EPSILON)
    normed = inputs * inv_rms
    scaled = normed * params[0]
    query_feat = scaled * params[1] + params[2]
    key_feat = scaled * params[3] + params[4]
    value_feat = scaled * params[5] + params[6]
    return (inv_rms, normed, scaled, query_feat, key_feat, value_feat)

def causal_filter(signal, taps):
    length, channels = signal.shape
    group_width = math.gcd(channels, 512)

    def per_group(both_parts):
        signal_part, taps_part = both_parts
        spectrum = jnp.fft.rfft(signal_part, 2 * length, axis=0) * jnp.fft.rfft(taps_part, 2 * length, axis=0)
        return jnp.fft.irfft(spectrum, 2 * length, axis=0)[:length]
    grouped_signal = signal.reshape(length, channels // group_width, group_width).transpose(1, 0, 2)
    grouped_taps = taps.reshape(length, channels // group_width, group_width).transpose(1, 0, 2)
    blocked = lax.map(per_group, (grouped_signal, grouped_taps))
    return blocked.transpose(1, 0, 2).reshape(length, channels).astype(jnp.float32)

def to_sequence(stored, span_order):
    blocks = stored.reshape(SPANS, TOK_DEV, stored.shape[-1])
    return jnp.zeros_like(blocks).at[span_order].set(blocks).reshape(SEQ_LEN, stored.shape[-1])

def to_storage(ordered, span_order):
    blocks = ordered.reshape(SPANS, TOK_DEV, ordered.shape[-1])
    return blocks[span_order].reshape(SEQ_LEN, ordered.shape[-1])

def reference(fwd_in, saved_in, saved_conv, grad_out, filters, mix_params, span_order):
    layer_outs = []
    input_grads = []
    param_grads = []
    for segment_index in range(SEGMENTS):
        params = mix_params[segment_index].astype(jnp.float32)
        taps = filters[segment_index].astype(jnp.float32)
        inputs = fwd_in[segment_index].astype(jnp.float32)
        inv_rms, normed, scaled, query_feat, key_feat, value_feat = mixer_fields(inputs, params)
        mixed = (key_feat * value_feat).astype(jnp.bfloat16)
        conv_seq = causal_filter(to_sequence(mixed, span_order).astype(jnp.float32), taps)
        conv = lax.optimization_barrier(to_storage(conv_seq, span_order).astype(jnp.bfloat16))
        layer_outs.append((inputs + query_feat * conv.astype(jnp.float32)).astype(jnp.bfloat16))
        saved = saved_in[segment_index].astype(jnp.float32)
        cotangent = grad_out[segment_index].astype(jnp.float32)
        inv_rms, normed, scaled, query_feat, key_feat, value_feat = mixer_fields(saved, params)
        grad_conv = (cotangent * query_feat).astype(jnp.bfloat16)
        grad_seq = to_sequence(grad_conv, span_order).astype(jnp.float32)
        grad_mixed_seq = causal_filter(grad_seq[::-1], taps)[::-1]
        grad_mixed = lax.optimization_barrier(to_storage(grad_mixed_seq, span_order).astype(jnp.bfloat16))
        grad_mixed = grad_mixed.astype(jnp.float32)
        grad_query = cotangent * saved_conv[segment_index].astype(jnp.float32)
        grad_key = grad_mixed * value_feat
        grad_value = grad_mixed * key_feat
        grad_scaled = grad_query * params[1] + grad_key * params[3] + grad_value * params[5]
        rows = jnp.stack([lax.optimization_barrier(jnp.sum(grad_scaled * normed, axis=0)), lax.optimization_barrier(jnp.sum(grad_query * scaled, axis=0)), lax.optimization_barrier(jnp.sum(grad_query, axis=0)), lax.optimization_barrier(jnp.sum(grad_key * scaled, axis=0)), lax.optimization_barrier(jnp.sum(grad_key, axis=0)), lax.optimization_barrier(jnp.sum(grad_value * scaled, axis=0)), lax.optimization_barrier(jnp.sum(grad_value, axis=0))])
        param_grads.append(rows)
        grad_normed = grad_scaled * params[0]
        cross = lax.optimization_barrier(jnp.mean(grad_normed * normed, axis=1, keepdims=True))
        input_grads.append((cotangent + inv_rms * (grad_normed - normed * cross)).astype(jnp.bfloat16))
    layer_out = jnp.stack(layer_outs)
    input_grad = jnp.stack(input_grads)
    param_grad = jnp.stack(param_grads)
    received = jnp.stack([input_grad[1], layer_out[0]])
    return (layer_out, input_grad, param_grad, received)
```

```python
import functools

import jax
import jax.numpy as jnp
import numpy as np
from jax import lax
from jax.experimental import pallas as pl
from jax.experimental.pallas import tpu as pltpu
from jax.sharding import PartitionSpec as P

EPSILON = 1e-05
MESH = pl.DeviceIdType.MESH


def transform_tables(rows):
    period = 2 * rows
    angle = (
        2.0 * np.pi / period * (np.arange(rows)[:, None] + 0.5) * np.arange(period)[None, :]
    )
    forward = np.concatenate([np.cos(angle), -np.sin(angle)], axis=0)
    inverse = (forward[:, rows:] / rows).T
    enter = np.stack([forward[:, :rows], inverse.T])
    leave = np.stack([inverse, forward[:, :rows].T])
    return tuple(jnp.asarray(t, jnp.bfloat16) for t in (forward, enter, leave))


def fold_lanes(values):
    lanes = 128
    total = values[:, :lanes]
    for at in range(lanes, values.shape[1], lanes):
        total = total + values[:, at : at + lanes]
    return total


def widen(column, width):
    return jnp.concatenate([column] * (width // column.shape[1]), axis=1)


def kernel(
    sizes,
    order,
    fwd_in,
    saved_in,
    saved_conv,
    grad_out,
    filters,
    params,
    forward_tab,
    enter_tab,
    leave_tab,
    layer_out,
    input_grad,
    param_grad,
    received,
    own_all,
    grad_all,
    spectra,
    grad_normed,
    column_all,
    saved_column,
    cross_lanes,
    square_rows,
    rms_rows,
    cross_rows,
    sum_rows,
    load_sem,
    send_sem,
    recv_sem,
    square_sem,
    rms_sem,
    cross_sem,
    sum_sem,
    relay_sem,
):
    n_seq, n_chan, channels, chunks = sizes
    rows, slab = saved_in.shape
    width = slab // chunks
    chips = n_seq // 2
    me = lax.axis_index("seq")
    my_chan = lax.axis_index("chan")
    pipe = lax.axis_index("pipe")
    chip, core = me // 2, me % 2
    sibling = chip * 2 + 1 - core

    def columns(c):
        return pl.ds(pl.multiple_of(c * width, width), width)

    def same_core(j):
        return lax.rem(chip + j, chips) * 2 + core

    def other_core(j):
        return lax.rem(chip + j, chips) * 2 + 1 - core

    def block_copy(kind, slot, c, k, target):
        buffer = own_all if kind == 0 else grad_all
        return pltpu.make_async_remote_copy(
            src_ref=buffer.at[slot, :, columns(c)],
            dst_ref=buffer.at[slot, :, columns(c)],
            send_sem=send_sem.at[kind, k, c],
            recv_sem=recv_sem.at[kind, slot, c],
            device_id={"seq": target},
            device_id_type=MESH,
        )

    def own_copies(kind, c):
        found = [block_copy(kind, me, c, j, same_core(j)) for j in range(1, chips)]
        return found + [block_copy(kind, me, c, 0, sibling)]

    def relay_copies(kind, c):
        return [
            block_copy(kind, same_core(j), c, chips - 1 + j, sibling) for j in range(1, chips)
        ]

    def start_own(kind, c):
        for copy in own_copies(kind, c):
            copy.start()

    def relay(kind, c):
        for j, copy in enumerate(relay_copies(kind, c)):
            block_copy(kind, same_core(j + 1), c, 0, sibling).wait_recv()
            copy.start()

    def arrive(kind, slot, c):
        block_copy(kind, slot, c, 0, sibling).wait_recv()

    def small_copies(buffer, sems, axis, index, count):
        return [
            pltpu.make_async_remote_copy(
                src_ref=buffer.at[index],
                dst_ref=buffer.at[index],
                send_sem=sems.at[0, j],
                recv_sem=sems.at[1, index],
                device_id={axis: lax.rem(index + j, count)},
                device_id_type=MESH,
            )
            for j in range(1, count)
        ]

    def small_wait(buffer, sems, axis, index, count):
        for j in range(1, count):
            peer = lax.rem(index + j, count)
            pltpu.make_async_remote_copy(
                src_ref=buffer.at[peer],
                dst_ref=buffer.at[peer],
                send_sem=sems.at[0, j],
                recv_sem=sems.at[1, peer],
                device_id={axis: peer},
                device_id_type=MESH,
            ).wait_recv()

    def partner_copy(source, c):
        return pltpu.make_async_remote_copy(
            src_ref=source.at[:, columns(c)],
            dst_ref=received.at[:, columns(c)],
            send_sem=relay_sem.at[0, c],
            recv_sem=relay_sem.at[1, c],
            device_id={"pipe": 1 - pipe},
            device_id_type=MESH,
        )

    def load_copy(c):
        return pltpu.make_async_copy(
            fwd_in.at[:, columns(c)], own_all.at[me, :, columns(c)], load_sem.at[c]
        )

    for c in range(chunks):
        load_copy(c).start()

    barrier = pltpu.get_barrier_semaphore()
    for j in range(1, n_seq):
        pl.semaphore_signal(
            barrier, inc=1, device_id={"seq": lax.rem(me + j, n_seq)}, device_id_type=MESH
        )
    for j in range(1, n_chan):
        pl.semaphore_signal(
            barrier, inc=1, device_id={"chan": lax.rem(my_chan + j, n_chan)}, device_id_type=MESH
        )
    pl.semaphore_signal(barrier, inc=1, device_id={"pipe": 1 - pipe}, device_id_type=MESH)
    pl.semaphore_wait(barrier, n_seq + n_chan - 1)

    early = chunks // 2
    for c in range(chunks):
        load_copy(c).wait()
        if c < early:
            start_own(0, c)

    def squares(read):
        def step(c, total):
            part = read(c).astype(jnp.float32)
            return total + fold_lanes(part * part)

        lanes = lax.fori_loop(0, chunks, step, jnp.zeros((rows, 128), jnp.float32))
        return jnp.sum(lanes.T, axis=0, keepdims=True)

    saved_row = squares(lambda c: saved_in[:, columns(c)])
    fwd_row = squares(lambda c: own_all[me, :, columns(c)])
    square_rows[my_chan] = jnp.concatenate([fwd_row, saved_row] * 4, axis=0)
    for copy in small_copies(square_rows, square_sem, "chan", my_chan, n_chan):
        copy.start()

    def filter_step(c, carry):
        cols = columns(c)
        spectra[0, :, cols] = jnp.zeros((2 * rows, width), jnp.bfloat16)
        spectra[1, :, cols] = jnp.dot(
            forward_tab[:, rows:], filters[:rows, cols], preferred_element_type=jnp.float32
        ).astype(jnp.bfloat16)

        def window(d, inner):
            taps = filters[pl.ds(pl.multiple_of((d - 1) * rows, rows), 2 * rows), cols]
            spectra[d + 1, :, cols] = jnp.dot(
                forward_tab[...], taps, preferred_element_type=jnp.float32
            ).astype(jnp.bfloat16)
            return inner

        return lax.fori_loop(1, n_seq, window, carry)

    lax.fori_loop(0, chunks, filter_step, 0)

    small_wait(square_rows, square_sem, "chan", my_chan, n_chan)
    total_squares = square_rows[0]
    for j in range(1, n_chan):
        total_squares = total_squares + square_rows[j]
    inv_rows = lax.rsqrt(total_squares / channels + EPSILON)
    rms_rows[me] = inv_rows
    for copy in small_copies(rms_rows, rms_sem, "seq", me, n_seq):
        copy.start()
    saved_column[...] = jnp.broadcast_to(inv_rows[1:2], (rows, rows)).T

    def param(index, cols):
        return params[index : index + 1, cols]

    def grad_conv_step(c, carry):
        cols = columns(c)
        scaled = (
            saved_in[:, cols].astype(jnp.float32) * widen(saved_column[...], width) * param(0, cols)
        )
        query = scaled * param(1, cols) + param(2, cols)
        grad_all[me, :, cols] = (grad_out[:, cols].astype(jnp.float32) * query).astype(jnp.bfloat16)
        start_own(1, c)
        return carry

    lax.fori_loop(0, chunks, grad_conv_step, 0)

    small_wait(rms_rows, rms_sem, "seq", me, n_seq)
    for s in range(n_seq):
        column_all[s] = jnp.broadcast_to(rms_rows[s, 0:1], (rows, rows)).T

    my_position = order[me]

    def long_conv(kind, c, signal):
        cols = columns(c)

        def term(slot, sums):
            distance = my_position - order[slot] if kind == 0 else order[slot] - my_position
            entering = jnp.dot(
                enter_tab[kind], signal(slot), preferred_element_type=jnp.float32
            )
            window = spectra[jnp.maximum(distance, -1) + 1, :, cols].astype(jnp.float32)
            data_real, data_imag = entering[:rows], entering[rows:]
            tap_real, tap_imag = window[:rows], window[rows:]
            if kind == 0:
                real = tap_real * data_real - tap_imag * data_imag
                imag = tap_real * data_imag + tap_imag * data_real
            else:
                real = tap_real * data_real + tap_imag * data_imag
                imag = tap_real * data_imag - tap_imag * data_real
            if sums is None:
                return real, imag
            return sums[0] + real, sums[1] + imag

        sums = term(me, None)
        arrive(kind, sibling, c)
        sums = term(sibling, sums)
        for j in range(1, chips):
            sums = term(same_core(j), sums)
        for j in range(1, chips):
            arrive(kind, other_core(j), c)
            sums = term(other_core(j), sums)
        spectrum = jnp.concatenate(sums, axis=0).astype(jnp.bfloat16)
        return jnp.dot(leave_tab[kind], spectrum, preferred_element_type=jnp.float32).astype(
            jnp.bfloat16
        )

    def backward_step(c, carry):
        cols = columns(c)
        relay(1, c)
        grad_mixed = long_conv(1, c, lambda slot: grad_all[slot, :, cols]).astype(jnp.float32)
        normed = saved_in[:, cols].astype(jnp.float32) * widen(saved_column[...], width)
        scaled = normed * param(0, cols)
        key = scaled * param(3, cols) + param(4, cols)
        value = scaled * param(5, cols) + param(6, cols)
        grad_query = grad_out[:, cols].astype(jnp.float32) * saved_conv[:, cols].astype(jnp.float32)
        grad_key = grad_mixed * value
        grad_value = grad_mixed * key
        grad_scaled = (
            grad_query * param(1, cols) + grad_key * param(3, cols) + grad_value * param(5, cols)
        )
        terms = [
            grad_scaled * normed,
            grad_query * scaled,
            grad_query,
            grad_key * scaled,
            grad_key,
            grad_value * scaled,
            grad_value,
        ]
        sums = [jnp.sum(term, axis=0, keepdims=True) for term in terms]
        sum_rows[me, :, cols] = jnp.concatenate(sums + sums[:1], axis=0)
        outer = grad_scaled * param(0, cols)
        grad_normed[:, cols] = outer
        cross_lanes[...] += fold_lanes(outer * normed)
        return carry

    cross_lanes[...] = jnp.zeros_like(cross_lanes)
    for c in range(early):
        relay(0, c)
    lax.fori_loop(0, early, backward_step, 0)
    for c in range(early, chunks):
        start_own(0, c)
    lax.fori_loop(early, chunks, backward_step, 0)

    cross_rows[my_chan] = jnp.broadcast_to(
        jnp.sum(cross_lanes[...].T, axis=0, keepdims=True), (8, rows)
    )
    for copy in small_copies(cross_rows, cross_sem, "chan", my_chan, n_chan):
        copy.start()
    for copy in small_copies(sum_rows, sum_sem, "seq", me, n_seq):
        copy.start()

    def forward_step(c, carry):
        cols = columns(c)

        def mixed(slot):
            scaled = (
                own_all[slot, :, cols].astype(jnp.float32)
                * widen(column_all[slot], width)
                * param(0, cols)
            )
            key = scaled * param(3, cols) + param(4, cols)
            value = scaled * param(5, cols) + param(6, cols)
            return (key * value).astype(jnp.bfloat16)

        conv = long_conv(0, c, mixed).astype(jnp.float32)
        inputs = own_all[me, :, cols].astype(jnp.float32)
        scaled = inputs * widen(column_all[me], width) * param(0, cols)
        query = scaled * param(1, cols) + param(2, cols)
        layer_out[:, cols] = (inputs + query * conv).astype(jnp.bfloat16)

        @pl.when(pipe == 0)
        def _():
            partner_copy(layer_out, c).start()

        return carry

    lax.fori_loop(0, early, forward_step, 0)

    small_wait(cross_rows, cross_sem, "chan", my_chan, n_chan)
    cross = cross_rows[0]
    for j in range(1, n_chan):
        cross = cross + cross_rows[j]
    cross_lanes[...] = jnp.broadcast_to(cross[0:1] / channels, (rows, rows)).T

    def input_grad_step(c, carry):
        cols = columns(c)
        inverse = widen(saved_column[...], width)
        normed = saved_in[:, cols].astype(jnp.float32) * inverse
        inner = grad_normed[:, cols] - normed * widen(cross_lanes[...], width)
        input_grad[:, cols] = (
            grad_out[:, cols].astype(jnp.float32) + inverse * inner
        ).astype(jnp.bfloat16)

        @pl.when(pipe == 1)
        def _():
            partner_copy(input_grad, c).start()

        return carry

    lax.fori_loop(0, chunks, input_grad_step, 0)

    for c in range(early, chunks):
        relay(0, c)
    lax.fori_loop(early, chunks, forward_step, 0)

    small_wait(sum_rows, sum_sem, "seq", me, n_seq)
    total = sum_rows[0]
    for s in range(1, n_seq):
        total = total + sum_rows[s]
    param_grad[...] = total[: param_grad.shape[0]]

    for c in range(chunks):
        for kind in range(2):
            for copy in own_copies(kind, c) + relay_copies(kind, c):
                copy.wait_send()
    for buffer, sems, axis, index, count in (
        (square_rows, square_sem, "chan", my_chan, n_chan),
        (cross_rows, cross_sem, "chan", my_chan, n_chan),
        (rms_rows, rms_sem, "seq", me, n_seq),
        (sum_rows, sum_sem, "seq", me, n_seq),
    ):
        for copy in small_copies(buffer, sems, axis, index, count):
            copy.wait_send()
    for c in range(chunks):
        partner_copy(layer_out, c).wait()


def per_device(n_seq, n_chan, fwd_in, saved_in, saved_conv, grad_out, filters, mix_params, order):
    rows, slab = fwd_in.shape[1:]
    chunks = 4
    sizes = (n_seq, n_chan, slab * n_chan, chunks)
    n_params = mix_params.shape[1]
    block = jax.ShapeDtypeStruct((rows, slab), jnp.bfloat16)
    vmem = pl.BlockSpec(memory_space=pltpu.VMEM)
    dma = pltpu.SemaphoreType.DMA
    outs = pl.pallas_call(
        functools.partial(kernel, sizes),
        out_shape=(block, block, jax.ShapeDtypeStruct((n_params, slab), jnp.float32), block),
        in_specs=[pl.BlockSpec(memory_space=pltpu.SMEM), pl.BlockSpec(memory_space=pl.ANY)]
        + [vmem] * 8,
        out_specs=(vmem,) * 4,
        scratch_shapes=[
            pltpu.VMEM((n_seq, rows, slab), jnp.bfloat16),
            pltpu.VMEM((n_seq, rows, slab), jnp.bfloat16),
            pltpu.VMEM((n_seq + 1, 2 * rows, slab), jnp.bfloat16),
            pltpu.VMEM((rows, slab), jnp.float32),
            pltpu.VMEM((n_seq, rows, 128), jnp.float32),
            pltpu.VMEM((rows, 128), jnp.float32),
            pltpu.VMEM((rows, 128), jnp.float32),
            pltpu.VMEM((n_chan, 8, rows), jnp.float32),
            pltpu.VMEM((n_seq, 8, rows), jnp.float32),
            pltpu.VMEM((n_chan, 8, rows), jnp.float32),
            pltpu.VMEM((n_seq, 8, slab), jnp.float32),
            dma((chunks,)),
            dma((2, n_seq, chunks)),
            dma((2, n_seq, chunks)),
            dma((2, n_chan)),
            dma((2, n_seq)),
            dma((2, n_chan)),
            dma((2, n_seq)),
            dma((2, chunks)),
        ],
        compiler_params=pltpu.CompilerParams(
            collective_id=0, has_side_effects=True, vmem_limit_bytes=60 * 2**20
        ),
    )(
        order,
        fwd_in[0],
        saved_in[0],
        saved_conv[0],
        grad_out[0],
        filters[0],
        mix_params[0],
        *transform_tables(rows),
    )
    layer_out, input_grad, param_grad, received = outs
    return (layer_out[None], input_grad[None], param_grad[None], received[None])


def solution(mesh):
    spread = P("pipe", "seq", "chan")
    shared = P("pipe", None, "chan")
    return jax.shard_map(
        functools.partial(per_device, mesh.shape["seq"], mesh.shape["chan"]),
        mesh=mesh,
        in_specs=(spread, spread, spread, spread, shared, shared, P()),
        out_specs=(spread, spread, shared, spread),
        check_vma=False,
    )
```

```python
import functools

import jax
import jax.numpy as jnp
import numpy as np
from jax import lax
from jax.experimental import pallas as pl
from jax.experimental.pallas import tpu as pltpu
from jax.sharding import PartitionSpec as P

EPSILON = 1e-05
MESH = pl.DeviceIdType.MESH


def transform_tables(rows):
    period = 2 * rows
    angle = (
        2.0 * np.pi / period * (np.arange(rows)[:, None] + 0.5) * np.arange(period)[None, :]
    )
    forward = np.concatenate([np.cos(angle), -np.sin(angle)], axis=0)
    inverse = (forward[:, rows:] / rows).T
    enter = np.stack([forward[:, :rows], inverse.T])
    leave = np.stack([inverse, forward[:, :rows].T])
    return tuple(jnp.asarray(t, jnp.bfloat16) for t in (forward, enter, leave))


def fold_lanes(values):
    lanes = 128
    total = values[:, :lanes]
    for at in range(lanes, values.shape[1], lanes):
        total = total + values[:, at : at + lanes]
    return total


def widen(column, width):
    return jnp.concatenate([column] * (width // column.shape[1]), axis=1)


def kernel(
    sizes,
    order,
    fwd_in,
    saved_in_hbm,
    saved_conv_hbm,
    grad_out_hbm,
    filters_hbm,
    params,
    forward_tab,
    enter_tab,
    leave_tab,
    layer_out,
    input_grad,
    param_grad,
    received,
    saved_in,
    saved_conv,
    grad_out,
    filters,
    own_all,
    grad_all,
    spectra,
    grad_normed,
    column_all,
    saved_column,
    cross_lanes,
    square_rows,
    rms_rows,
    cross_rows,
    sum_rows,
    load_sem,
    operand_sem,
    send_sem,
    recv_sem,
    square_sem,
    rms_sem,
    cross_sem,
    sum_sem,
    relay_sem,
):
    n_seq, n_chan, channels, chunks = sizes
    rows, slab = saved_in.shape
    width = slab // chunks
    chips = n_seq // 2
    me = lax.axis_index("seq")
    my_chan = lax.axis_index("chan")
    pipe = lax.axis_index("pipe")
    chip, core = me // 2, me % 2
    sibling = chip * 2 + 1 - core

    def columns(c):
        return pl.ds(pl.multiple_of(c * width, width), width)

    def same_core(j):
        return lax.rem(chip + j, chips) * 2 + core

    def other_core(j):
        return lax.rem(chip + j, chips) * 2 + 1 - core

    def block_copy(kind, slot, c, k, target):
        buffer = own_all if kind == 0 else grad_all
        return pltpu.make_async_remote_copy(
            src_ref=buffer.at[slot, :, columns(c)],
            dst_ref=buffer.at[slot, :, columns(c)],
            send_sem=send_sem.at[kind, k, c],
            recv_sem=recv_sem.at[kind, slot, c],
            device_id={"seq": target},
            device_id_type=MESH,
        )

    def own_copies(kind, c):
        found = [block_copy(kind, me, c, j, same_core(j)) for j in range(1, chips)]
        return found + [block_copy(kind, me, c, 0, sibling)]

    def relay_copies(kind, c):
        return [
            block_copy(kind, same_core(j), c, chips - 1 + j, sibling) for j in range(1, chips)
        ]

    def start_own(kind, c):
        for copy in own_copies(kind, c):
            copy.start()

    def relay(kind, c):
        for j, copy in enumerate(relay_copies(kind, c)):
            block_copy(kind, same_core(j + 1), c, 0, sibling).wait_recv()
            copy.start()

    def arrive(kind, slot, c):
        block_copy(kind, slot, c, 0, sibling).wait_recv()

    def small_copies(buffer, sems, axis, index, count):
        return [
            pltpu.make_async_remote_copy(
                src_ref=buffer.at[index],
                dst_ref=buffer.at[index],
                send_sem=sems.at[0, j],
                recv_sem=sems.at[1, index],
                device_id={axis: lax.rem(index + j, count)},
                device_id_type=MESH,
            )
            for j in range(1, count)
        ]

    def small_wait(buffer, sems, axis, index, count):
        for j in range(1, count):
            peer = lax.rem(index + j, count)
            pltpu.make_async_remote_copy(
                src_ref=buffer.at[peer],
                dst_ref=buffer.at[peer],
                send_sem=sems.at[0, j],
                recv_sem=sems.at[1, peer],
                device_id={axis: peer},
                device_id_type=MESH,
            ).wait_recv()

    def partner_copy(source, c):
        return pltpu.make_async_remote_copy(
            src_ref=source.at[:, columns(c)],
            dst_ref=received.at[:, columns(c)],
            send_sem=relay_sem.at[0, c],
            recv_sem=relay_sem.at[1, c],
            device_id={"pipe": 1 - pipe},
            device_id_type=MESH,
        )

    def load_copy(c):
        return pltpu.make_async_copy(
            fwd_in.at[:, columns(c)], own_all.at[me, :, columns(c)], load_sem.at[c]
        )

    operands = [
        pltpu.make_async_copy(source, target, operand_sem.at[i])
        for i, (source, target) in enumerate(
            (
                (saved_in_hbm, saved_in),
                (filters_hbm, filters),
                (grad_out_hbm, grad_out),
                (saved_conv_hbm, saved_conv),
            )
        )
    ]
    for c in range(chunks):
        load_copy(c).start()
    for copy in operands:
        copy.start()

    barrier = pltpu.get_barrier_semaphore()
    for j in range(1, n_seq):
        pl.semaphore_signal(
            barrier, inc=1, device_id={"seq": lax.rem(me + j, n_seq)}, device_id_type=MESH
        )
    for j in range(1, n_chan):
        pl.semaphore_signal(
            barrier, inc=1, device_id={"chan": lax.rem(my_chan + j, n_chan)}, device_id_type=MESH
        )
    pl.semaphore_signal(barrier, inc=1, device_id={"pipe": 1 - pipe}, device_id_type=MESH)
    pl.semaphore_wait(barrier, n_seq + n_chan - 1)

    early = chunks // 2
    for c in range(chunks):
        load_copy(c).wait()
        if c < early:
            start_own(0, c)

    def squares(read):
        def step(c, total):
            part = read(c).astype(jnp.float32)
            return total + fold_lanes(part * part)

        lanes = lax.fori_loop(0, chunks, step, jnp.zeros((rows, 128), jnp.float32))
        return jnp.sum(lanes.T, axis=0, keepdims=True)

    fwd_row = squares(lambda c: own_all[me, :, columns(c)])
    operands[0].wait()
    saved_row = squares(lambda c: saved_in[:, columns(c)])
    square_rows[my_chan] = jnp.concatenate([fwd_row, saved_row] * 4, axis=0)
    for copy in small_copies(square_rows, square_sem, "chan", my_chan, n_chan):
        copy.start()

    def filter_step(c, carry):
        cols = columns(c)
        spectra[0, :, cols] = jnp.zeros((2 * rows, width), jnp.bfloat16)
        spectra[1, :, cols] = jnp.dot(
            forward_tab[:, rows:], filters[:rows, cols], preferred_element_type=jnp.float32
        ).astype(jnp.bfloat16)

        def window(d, inner):
            taps = filters[pl.ds(pl.multiple_of((d - 1) * rows, rows), 2 * rows), cols]
            spectra[d + 1, :, cols] = jnp.dot(
                forward_tab[...], taps, preferred_element_type=jnp.float32
            ).astype(jnp.bfloat16)
            return inner

        return lax.fori_loop(1, n_seq, window, carry)

    operands[1].wait()
    lax.fori_loop(0, chunks, filter_step, 0)

    small_wait(square_rows, square_sem, "chan", my_chan, n_chan)
    total_squares = square_rows[0]
    for j in range(1, n_chan):
        total_squares = total_squares + square_rows[j]
    inv_rows = lax.rsqrt(total_squares / channels + EPSILON)
    rms_rows[me] = inv_rows
    for copy in small_copies(rms_rows, rms_sem, "seq", me, n_seq):
        copy.start()
    saved_column[...] = jnp.broadcast_to(inv_rows[1:2], (rows, rows)).T

    def param(index, cols):
        return params[index, :, cols]

    def grad_conv_step(c, carry):
        cols = columns(c)
        scaled = (
            saved_in[:, cols].astype(jnp.float32) * widen(saved_column[...], width) * param(0, cols)
        )
        query = scaled * param(1, cols) + param(2, cols)
        grad_all[me, :, cols] = (grad_out[:, cols].astype(jnp.float32) * query).astype(jnp.bfloat16)
        start_own(1, c)
        return carry

    operands[2].wait()
    lax.fori_loop(0, chunks, grad_conv_step, 0)
    operands[3].wait()

    small_wait(rms_rows, rms_sem, "seq", me, n_seq)
    for s in range(n_seq):
        column_all[s] = jnp.broadcast_to(rms_rows[s, 0:1], (rows, rows)).T

    my_position = order[me]

    def long_conv(kind, c, signal):
        cols = columns(c)

        def term(slot, sums):
            distance = my_position - order[slot] if kind == 0 else order[slot] - my_position
            entering = jnp.dot(
                enter_tab[kind], signal(slot), preferred_element_type=jnp.float32
            )
            window = spectra[jnp.maximum(distance, -1) + 1, :, cols].astype(jnp.float32)
            data_real, data_imag = entering[:rows], entering[rows:]
            tap_real, tap_imag = window[:rows], window[rows:]
            if kind == 0:
                real = tap_real * data_real - tap_imag * data_imag
                imag = tap_real * data_imag + tap_imag * data_real
            else:
                real = tap_real * data_real + tap_imag * data_imag
                imag = tap_real * data_imag - tap_imag * data_real
            if sums is None:
                return real, imag
            return sums[0] + real, sums[1] + imag

        sums = term(me, None)
        arrive(kind, sibling, c)
        sums = term(sibling, sums)
        for j in range(1, chips):
            sums = term(same_core(j), sums)
        for j in range(1, chips):
            arrive(kind, other_core(j), c)
            sums = term(other_core(j), sums)
        spectrum = jnp.concatenate(sums, axis=0).astype(jnp.bfloat16)
        return jnp.dot(leave_tab[kind], spectrum, preferred_element_type=jnp.float32).astype(
            jnp.bfloat16
        )

    def backward_step(c, carry):
        cols = columns(c)
        relay(1, c)
        grad_mixed = long_conv(1, c, lambda slot: grad_all[slot, :, cols]).astype(jnp.float32)
        normed = saved_in[:, cols].astype(jnp.float32) * widen(saved_column[...], width)
        scaled = normed * param(0, cols)
        key = scaled * param(3, cols) + param(4, cols)
        value = scaled * param(5, cols) + param(6, cols)
        grad_query = grad_out[:, cols].astype(jnp.float32) * saved_conv[:, cols].astype(jnp.float32)
        grad_key = grad_mixed * value
        grad_value = grad_mixed * key
        grad_scaled = (
            grad_query * param(1, cols) + grad_key * param(3, cols) + grad_value * param(5, cols)
        )
        terms = [
            grad_scaled * normed,
            grad_query * scaled,
            grad_query,
            grad_key * scaled,
            grad_key,
            grad_value * scaled,
            grad_value,
        ]
        sums = [jnp.sum(term, axis=0, keepdims=True) for term in terms]
        sum_rows[me, :, cols] = jnp.concatenate(sums + sums[:1], axis=0)
        outer = grad_scaled * param(0, cols)
        grad_normed[:, cols] = outer
        cross_lanes[...] += fold_lanes(outer * normed)
        return carry

    cross_lanes[...] = jnp.zeros_like(cross_lanes)
    for c in range(early):
        relay(0, c)
    lax.fori_loop(0, early, backward_step, 0)
    for c in range(early, chunks):
        start_own(0, c)
    lax.fori_loop(early, chunks, backward_step, 0)

    cross_rows[my_chan] = jnp.broadcast_to(
        jnp.sum(cross_lanes[...].T, axis=0, keepdims=True), (8, rows)
    )
    for copy in small_copies(cross_rows, cross_sem, "chan", my_chan, n_chan):
        copy.start()
    for copy in small_copies(sum_rows, sum_sem, "seq", me, n_seq):
        copy.start()

    def forward_step(c, carry):
        cols = columns(c)

        def mixed(slot):
            scaled = (
                own_all[slot, :, cols].astype(jnp.float32)
                * widen(column_all[slot], width)
                * param(0, cols)
            )
            key = scaled * param(3, cols) + param(4, cols)
            value = scaled * param(5, cols) + param(6, cols)
            return (key * value).astype(jnp.bfloat16)

        conv = long_conv(0, c, mixed).astype(jnp.float32)
        inputs = own_all[me, :, cols].astype(jnp.float32)
        scaled = inputs * widen(column_all[me], width) * param(0, cols)
        query = scaled * param(1, cols) + param(2, cols)
        layer_out[:, cols] = (inputs + query * conv).astype(jnp.bfloat16)

        @pl.when(pipe == 0)
        def _():
            partner_copy(layer_out, c).start()

        return carry

    lax.fori_loop(0, early, forward_step, 0)

    small_wait(cross_rows, cross_sem, "chan", my_chan, n_chan)
    cross = cross_rows[0]
    for j in range(1, n_chan):
        cross = cross + cross_rows[j]
    cross_lanes[...] = jnp.broadcast_to(cross[0:1] / channels, (rows, rows)).T

    def input_grad_step(c, carry):
        cols = columns(c)
        inverse = widen(saved_column[...], width)
        normed = saved_in[:, cols].astype(jnp.float32) * inverse
        inner = grad_normed[:, cols] - normed * widen(cross_lanes[...], width)
        input_grad[:, cols] = (
            grad_out[:, cols].astype(jnp.float32) + inverse * inner
        ).astype(jnp.bfloat16)

        @pl.when(pipe == 1)
        def _():
            partner_copy(input_grad, c).start()

        return carry

    lax.fori_loop(0, chunks, input_grad_step, 0)

    for c in range(early, chunks):
        relay(0, c)
    lax.fori_loop(early, chunks, forward_step, 0)

    small_wait(sum_rows, sum_sem, "seq", me, n_seq)
    total = sum_rows[0]
    for s in range(1, n_seq):
        total = total + sum_rows[s]
    for i in range(param_grad.shape[0]):
        param_grad[i] = total[i : i + 1]

    for c in range(chunks):
        for kind in range(2):
            for copy in own_copies(kind, c) + relay_copies(kind, c):
                copy.wait_send()
    for buffer, sems, axis, index, count in (
        (square_rows, square_sem, "chan", my_chan, n_chan),
        (cross_rows, cross_sem, "chan", my_chan, n_chan),
        (rms_rows, rms_sem, "seq", me, n_seq),
        (sum_rows, sum_sem, "seq", me, n_seq),
    ):
        for copy in small_copies(buffer, sems, axis, index, count):
            copy.wait_send()
    for c in range(chunks):
        partner_copy(layer_out, c).wait()


def store_kernel(count, *refs):
    copies = [
        pltpu.make_async_copy(refs[i], refs[count + i], refs[2 * count].at[i]) for i in range(count)
    ]
    for copy in copies:
        copy.start()
    for copy in copies:
        copy.wait()


def store(*arrays):
    count = len(arrays)
    anywhere = pl.BlockSpec(memory_space=pl.ANY)
    return pl.pallas_call(
        functools.partial(store_kernel, count),
        out_shape=tuple(jax.ShapeDtypeStruct(a.shape, a.dtype) for a in arrays),
        in_specs=[anywhere] * count,
        out_specs=(anywhere,) * count,
        scratch_shapes=[pltpu.SemaphoreType.DMA((count,))],
    )(*arrays)


def per_device(n_seq, n_chan, fwd_in, saved_in, saved_conv, grad_out, filters, mix_params, order):
    rows, slab = fwd_in.shape[1:]
    chunks = 4
    sizes = (n_seq, n_chan, slab * n_chan, chunks)
    n_params = mix_params.shape[1]
    block = jax.ShapeDtypeStruct((rows, slab), jnp.bfloat16)
    vmem = pl.BlockSpec(memory_space=pltpu.VMEM)
    dma = pltpu.SemaphoreType.DMA
    outs = pl.pallas_call(
        functools.partial(kernel, sizes),
        out_shape=(block, block, jax.ShapeDtypeStruct((n_params, 1, slab), jnp.float32), block),
        in_specs=[pl.BlockSpec(memory_space=pltpu.SMEM)]
        + [pl.BlockSpec(memory_space=pl.ANY)] * 5
        + [vmem] * 4,
        out_specs=(vmem,) * 4,
        scratch_shapes=[
            pltpu.VMEM((rows, slab), jnp.bfloat16),
            pltpu.VMEM((rows, slab), jnp.bfloat16),
            pltpu.VMEM((rows, slab), jnp.bfloat16),
            pltpu.VMEM(filters.shape[1:], jnp.bfloat16),
            pltpu.VMEM((n_seq, rows, slab), jnp.bfloat16),
            pltpu.VMEM((n_seq, rows, slab), jnp.bfloat16),
            pltpu.VMEM((n_seq + 1, 2 * rows, slab), jnp.bfloat16),
            pltpu.VMEM((rows, slab), jnp.float32),
            pltpu.VMEM((n_seq, rows, 128), jnp.float32),
            pltpu.VMEM((rows, 128), jnp.float32),
            pltpu.VMEM((rows, 128), jnp.float32),
            pltpu.VMEM((n_chan, 8, rows), jnp.float32),
            pltpu.VMEM((n_seq, 8, rows), jnp.float32),
            pltpu.VMEM((n_chan, 8, rows), jnp.float32),
            pltpu.VMEM((n_seq, 8, slab), jnp.float32),
            dma((chunks,)),
            dma((4,)),
            dma((2, n_seq, chunks)),
            dma((2, n_seq, chunks)),
            dma((2, n_chan)),
            dma((2, n_seq)),
            dma((2, n_chan)),
            dma((2, n_seq)),
            dma((2, chunks)),
        ],
        compiler_params=pltpu.CompilerParams(
            collective_id=0, has_side_effects=True, vmem_limit_bytes=60 * 2**20
        ),
    )(
        order,
        fwd_in[0],
        saved_in[0],
        saved_conv[0],
        grad_out[0],
        filters[0],
        mix_params.transpose(1, 0, 2),
        *transform_tables(rows),
    )
    layer_out, input_grad, param_grad, received = store(*outs)
    return (layer_out[None], input_grad[None], param_grad.transpose(1, 0, 2), received[None])


def solution(mesh):
    spread = P("pipe", "seq", "chan")
    shared = P("pipe", None, "chan")
    return jax.shard_map(
        functools.partial(per_device, mesh.shape["seq"], mesh.shape["chan"]),
        mesh=mesh,
        in_specs=(spread, spread, spread, spread, shared, shared, P()),
        out_specs=(spread, spread, shared, spread),
        check_vma=False,
    )
```

```python
import functools

import jax
import jax.numpy as jnp
import numpy as np
from jax import lax
from jax.experimental import pallas as pl
from jax.experimental.pallas import tpu as pltpu
from jax.sharding import PartitionSpec as P

EPSILON = 1e-05
MESH = pl.DeviceIdType.MESH


def transform_tables(rows):
    period = 2 * rows
    angle = (
        2.0 * np.pi / period * (np.arange(rows)[:, None] + 0.5) * np.arange(period)[None, :]
    )
    forward = np.concatenate([np.cos(angle), -np.sin(angle)], axis=0)
    inverse = (forward[:, rows:] / rows).T
    enter = np.stack([forward[:, :rows], inverse.T])
    leave = np.stack([inverse, forward[:, :rows].T])
    return tuple(jnp.asarray(t, jnp.bfloat16) for t in (forward, enter, leave))


def fold_lanes(values):
    lanes = 128
    total = values[:, :lanes]
    for at in range(lanes, values.shape[1], lanes):
        total = total + values[:, at : at + lanes]
    return total


def widen(column, width):
    return jnp.concatenate([column] * (width // column.shape[1]), axis=1)


def kernel(
    sizes,
    order,
    fwd_in,
    saved_in_hbm,
    saved_conv_hbm,
    grad_out_hbm,
    filters_hbm,
    params,
    forward_tab,
    enter_tab,
    leave_tab,
    layer_out_hbm,
    input_grad_hbm,
    param_grad,
    received,
    layer_out,
    input_grad,
    saved_in,
    saved_conv,
    grad_out,
    filters,
    own_all,
    grad_all,
    spectra,
    grad_normed,
    column_all,
    saved_column,
    cross_lanes,
    square_rows,
    rms_rows,
    cross_rows,
    sum_rows,
    load_sem,
    operand_sem,
    result_sem,
    send_sem,
    recv_sem,
    square_sem,
    rms_sem,
    cross_sem,
    sum_sem,
    relay_sem,
):
    n_seq, n_chan, channels, chunks = sizes
    rows, slab = saved_in.shape
    width = slab // chunks
    chips = n_seq // 2
    me = lax.axis_index("seq")
    my_chan = lax.axis_index("chan")
    pipe = lax.axis_index("pipe")
    chip, core = me // 2, me % 2
    sibling = chip * 2 + 1 - core

    def columns(c):
        return pl.ds(pl.multiple_of(c * width, width), width)

    def same_core(j):
        return lax.rem(chip + j, chips) * 2 + core

    def other_core(j):
        return lax.rem(chip + j, chips) * 2 + 1 - core

    def block_copy(kind, slot, c, k, target):
        buffer = own_all if kind == 0 else grad_all
        return pltpu.make_async_remote_copy(
            src_ref=buffer.at[slot, :, columns(c)],
            dst_ref=buffer.at[slot, :, columns(c)],
            send_sem=send_sem.at[kind, k, c],
            recv_sem=recv_sem.at[kind, slot, c],
            device_id={"seq": target},
            device_id_type=MESH,
        )

    def own_copies(kind, c):
        found = [block_copy(kind, me, c, j, same_core(j)) for j in range(1, chips)]
        return found + [block_copy(kind, me, c, 0, sibling)]

    def relay_copies(kind, c):
        return [
            block_copy(kind, same_core(j), c, chips - 1 + j, sibling) for j in range(1, chips)
        ]

    def start_own(kind, c):
        for copy in own_copies(kind, c):
            copy.start()

    def relay(kind, c):
        for j, copy in enumerate(relay_copies(kind, c)):
            block_copy(kind, same_core(j + 1), c, 0, sibling).wait_recv()
            copy.start()

    def arrive(kind, slot, c):
        block_copy(kind, slot, c, 0, sibling).wait_recv()

    def small_copies(buffer, sems, axis, index, count):
        return [
            pltpu.make_async_remote_copy(
                src_ref=buffer.at[index],
                dst_ref=buffer.at[index],
                send_sem=sems.at[0, j],
                recv_sem=sems.at[1, index],
                device_id={axis: lax.rem(index + j, count)},
                device_id_type=MESH,
            )
            for j in range(1, count)
        ]

    def small_wait(buffer, sems, axis, index, count):
        for j in range(1, count):
            peer = lax.rem(index + j, count)
            pltpu.make_async_remote_copy(
                src_ref=buffer.at[peer],
                dst_ref=buffer.at[peer],
                send_sem=sems.at[0, j],
                recv_sem=sems.at[1, peer],
                device_id={axis: peer},
                device_id_type=MESH,
            ).wait_recv()

    def partner_copy(source, c):
        return pltpu.make_async_remote_copy(
            src_ref=source.at[:, columns(c)],
            dst_ref=received.at[:, columns(c)],
            send_sem=relay_sem.at[0, c],
            recv_sem=relay_sem.at[1, c],
            device_id={"pipe": 1 - pipe},
            device_id_type=MESH,
        )

    def load_copy(c):
        return pltpu.make_async_copy(
            fwd_in.at[:, columns(c)], own_all.at[me, :, columns(c)], load_sem.at[c]
        )

    operands = [
        pltpu.make_async_copy(source, target, operand_sem.at[i])
        for i, (source, target) in enumerate(
            (
                (saved_in_hbm, saved_in),
                (filters_hbm, filters),
                (grad_out_hbm, grad_out),
                (saved_conv_hbm, saved_conv),
            )
        )
    ]
    for c in range(chunks):
        load_copy(c).start()
    for copy in operands:
        copy.start()

    barrier = pltpu.get_barrier_semaphore()
    for j in range(1, n_seq):
        pl.semaphore_signal(
            barrier, inc=1, device_id={"seq": lax.rem(me + j, n_seq)}, device_id_type=MESH
        )
    for j in range(1, n_chan):
        pl.semaphore_signal(
            barrier, inc=1, device_id={"chan": lax.rem(my_chan + j, n_chan)}, device_id_type=MESH
        )
    pl.semaphore_signal(barrier, inc=1, device_id={"pipe": 1 - pipe}, device_id_type=MESH)
    pl.semaphore_wait(barrier, n_seq + n_chan - 1)

    early = chunks // 4
    middle = chunks // 2
    for c in range(chunks):
        load_copy(c).wait()
        if c < early:
            start_own(0, c)

    def squares(read):
        def step(c, total):
            part = read(c).astype(jnp.float32)
            return total + fold_lanes(part * part)

        lanes = lax.fori_loop(0, chunks, step, jnp.zeros((rows, 128), jnp.float32))
        return jnp.sum(lanes.T, axis=0, keepdims=True)

    fwd_row = squares(lambda c: own_all[me, :, columns(c)])
    operands[0].wait()
    saved_row = squares(lambda c: saved_in[:, columns(c)])
    square_rows[my_chan] = jnp.concatenate([fwd_row, saved_row] * 4, axis=0)
    for copy in small_copies(square_rows, square_sem, "chan", my_chan, n_chan):
        copy.start()

    def filter_step(c, carry):
        cols = columns(c)
        spectra[0, :, cols] = jnp.zeros((2 * rows, width), jnp.bfloat16)
        spectra[1, :, cols] = jnp.dot(
            forward_tab[:, rows:], filters[:rows, cols], preferred_element_type=jnp.float32
        ).astype(jnp.bfloat16)

        def window(d, inner):
            taps = filters[pl.ds(pl.multiple_of((d - 1) * rows, rows), 2 * rows), cols]
            spectra[d + 1, :, cols] = jnp.dot(
                forward_tab[...], taps, preferred_element_type=jnp.float32
            ).astype(jnp.bfloat16)
            return inner

        return lax.fori_loop(1, n_seq, window, carry)

    operands[1].wait()
    lax.fori_loop(0, middle, filter_step, 0)

    small_wait(square_rows, square_sem, "chan", my_chan, n_chan)
    total_squares = square_rows[0]
    for j in range(1, n_chan):
        total_squares = total_squares + square_rows[j]
    inv_rows = lax.rsqrt(total_squares / channels + EPSILON)
    rms_rows[me] = inv_rows
    for copy in small_copies(rms_rows, rms_sem, "seq", me, n_seq):
        copy.start()
    saved_column[...] = jnp.broadcast_to(inv_rows[1:2], (rows, rows)).T

    def param(index, cols):
        return params[index, :, cols]

    def grad_conv_step(c, carry):
        cols = columns(c)
        scaled = (
            saved_in[:, cols].astype(jnp.float32) * widen(saved_column[...], width) * param(0, cols)
        )
        query = scaled * param(1, cols) + param(2, cols)
        grad_all[me, :, cols] = (grad_out[:, cols].astype(jnp.float32) * query).astype(jnp.bfloat16)
        start_own(1, c)
        return carry

    operands[2].wait()
    lax.fori_loop(0, chunks, grad_conv_step, 0)
    lax.fori_loop(middle, chunks, filter_step, 0)
    operands[3].wait()

    small_wait(rms_rows, rms_sem, "seq", me, n_seq)
    for s in range(n_seq):
        column_all[s] = jnp.broadcast_to(rms_rows[s, 0:1], (rows, rows)).T

    my_position = order[me]

    def long_conv(kind, c, signal):
        cols = columns(c)

        def term(slot, sums):
            distance = my_position - order[slot] if kind == 0 else order[slot] - my_position
            entering = jnp.dot(
                enter_tab[kind], signal(slot), preferred_element_type=jnp.float32
            )
            window = spectra[jnp.maximum(distance, -1) + 1, :, cols].astype(jnp.float32)
            data_real, data_imag = entering[:rows], entering[rows:]
            tap_real, tap_imag = window[:rows], window[rows:]
            if kind == 0:
                real = tap_real * data_real - tap_imag * data_imag
                imag = tap_real * data_imag + tap_imag * data_real
            else:
                real = tap_real * data_real + tap_imag * data_imag
                imag = tap_real * data_imag - tap_imag * data_real
            if sums is None:
                return real, imag
            return sums[0] + real, sums[1] + imag

        sums = term(me, None)
        arrive(kind, sibling, c)
        sums = term(sibling, sums)
        for j in range(1, chips):
            sums = term(same_core(j), sums)
        for j in range(1, chips):
            arrive(kind, other_core(j), c)
            sums = term(other_core(j), sums)
        spectrum = jnp.concatenate(sums, axis=0).astype(jnp.bfloat16)
        return jnp.dot(leave_tab[kind], spectrum, preferred_element_type=jnp.float32).astype(
            jnp.bfloat16
        )

    def backward_step(c, carry):
        cols = columns(c)
        relay(1, c)
        grad_mixed = long_conv(1, c, lambda slot: grad_all[slot, :, cols]).astype(jnp.float32)
        normed = saved_in[:, cols].astype(jnp.float32) * widen(saved_column[...], width)
        scaled = normed * param(0, cols)
        key = scaled * param(3, cols) + param(4, cols)
        value = scaled * param(5, cols) + param(6, cols)
        grad_query = grad_out[:, cols].astype(jnp.float32) * saved_conv[:, cols].astype(jnp.float32)
        grad_key = grad_mixed * value
        grad_value = grad_mixed * key
        grad_scaled = (
            grad_query * param(1, cols) + grad_key * param(3, cols) + grad_value * param(5, cols)
        )
        terms = [
            grad_scaled * normed,
            grad_query * scaled,
            grad_query,
            grad_key * scaled,
            grad_key,
            grad_value * scaled,
            grad_value,
        ]
        sums = [jnp.sum(term, axis=0, keepdims=True) for term in terms]
        sum_rows[me, :, cols] = jnp.concatenate(sums + sums[:1], axis=0)
        outer = grad_scaled * param(0, cols)
        grad_normed[:, cols] = outer
        cross_lanes[...] += fold_lanes(outer * normed)
        return carry

    cross_lanes[...] = jnp.zeros_like(cross_lanes)
    for c in range(early):
        relay(0, c)
    lax.fori_loop(0, middle, backward_step, 0)
    for c in range(early, chunks):
        start_own(0, c)
    lax.fori_loop(middle, chunks, backward_step, 0)

    cross_rows[my_chan] = jnp.broadcast_to(
        jnp.sum(cross_lanes[...].T, axis=0, keepdims=True), (8, rows)
    )
    for copy in small_copies(cross_rows, cross_sem, "chan", my_chan, n_chan):
        copy.start()
    for copy in small_copies(sum_rows, sum_sem, "seq", me, n_seq):
        copy.start()

    def forward_step(c, carry):
        cols = columns(c)

        def mixed(slot):
            scaled = (
                own_all[slot, :, cols].astype(jnp.float32)
                * widen(column_all[slot], width)
                * param(0, cols)
            )
            key = scaled * param(3, cols) + param(4, cols)
            value = scaled * param(5, cols) + param(6, cols)
            return (key * value).astype(jnp.bfloat16)

        conv = long_conv(0, c, mixed).astype(jnp.float32)
        inputs = own_all[me, :, cols].astype(jnp.float32)
        scaled = inputs * widen(column_all[me], width) * param(0, cols)
        query = scaled * param(1, cols) + param(2, cols)
        layer_out[:, cols] = (inputs + query * conv).astype(jnp.bfloat16)

        @pl.when(pipe == 0)
        def _():
            partner_copy(layer_out, c).start()

        return carry

    lax.fori_loop(0, early, forward_step, 0)

    small_wait(cross_rows, cross_sem, "chan", my_chan, n_chan)
    cross = cross_rows[0]
    for j in range(1, n_chan):
        cross = cross + cross_rows[j]
    cross_lanes[...] = jnp.broadcast_to(cross[0:1] / channels, (rows, rows)).T

    def input_grad_step(c, carry):
        cols = columns(c)
        inverse = widen(saved_column[...], width)
        normed = saved_in[:, cols].astype(jnp.float32) * inverse
        inner = grad_normed[:, cols] - normed * widen(cross_lanes[...], width)
        input_grad[:, cols] = (
            grad_out[:, cols].astype(jnp.float32) + inverse * inner
        ).astype(jnp.bfloat16)

        @pl.when(pipe == 1)
        def _():
            partner_copy(input_grad, c).start()

        return carry

    lax.fori_loop(0, chunks, input_grad_step, 0)
    stores = [
        pltpu.make_async_copy(input_grad, input_grad_hbm, result_sem.at[0]),
        pltpu.make_async_copy(layer_out, layer_out_hbm, result_sem.at[1]),
    ]
    stores[0].start()

    def late_forward_step(c, carry):
        @pl.when(c + 1 < chunks)
        def _():
            relay(0, c + 1)

        return forward_step(c, carry)

    relay(0, early)
    lax.fori_loop(early, chunks, late_forward_step, 0)
    stores[1].start()

    small_wait(sum_rows, sum_sem, "seq", me, n_seq)
    total = sum_rows[0]
    for s in range(1, n_seq):
        total = total + sum_rows[s]
    for i in range(param_grad.shape[0]):
        param_grad[i] = total[i : i + 1]

    for c in range(chunks):
        for kind in range(2):
            for copy in own_copies(kind, c) + relay_copies(kind, c):
                copy.wait_send()
    for buffer, sems, axis, index, count in (
        (square_rows, square_sem, "chan", my_chan, n_chan),
        (cross_rows, cross_sem, "chan", my_chan, n_chan),
        (rms_rows, rms_sem, "seq", me, n_seq),
        (sum_rows, sum_sem, "seq", me, n_seq),
    ):
        for copy in small_copies(buffer, sems, axis, index, count):
            copy.wait_send()
    for c in range(chunks):
        partner_copy(layer_out, c).wait()
    for copy in stores:
        copy.wait()


def store_kernel(count, *refs):
    sources, targets, held = (refs[at * count : (at + 1) * count] for at in range(3))
    sems = refs[3 * count]
    fetches = [pltpu.make_async_copy(sources[i], held[i], sems.at[0, i]) for i in range(count)]
    stores = [pltpu.make_async_copy(held[i], targets[i], sems.at[1, i]) for i in range(count)]
    for copy in fetches:
        copy.start()
    for fetch, copy in zip(fetches, stores):
        fetch.wait()
        copy.start()
    for copy in stores:
        copy.wait()


def store(*arrays):
    count = len(arrays)
    anywhere = pl.BlockSpec(memory_space=pl.ANY)
    return pl.pallas_call(
        functools.partial(store_kernel, count),
        out_shape=tuple(jax.ShapeDtypeStruct(a.shape, a.dtype) for a in arrays),
        in_specs=[anywhere] * count,
        out_specs=(anywhere,) * count,
        scratch_shapes=[pltpu.VMEM(a.shape, a.dtype) for a in arrays]
        + [pltpu.SemaphoreType.DMA((2, count))],
    )(*arrays)


def per_device(n_seq, n_chan, fwd_in, saved_in, saved_conv, grad_out, filters, mix_params, order):
    rows, slab = fwd_in.shape[1:]
    chunks = 8
    sizes = (n_seq, n_chan, slab * n_chan, chunks)
    n_params = mix_params.shape[1]
    block = jax.ShapeDtypeStruct((rows, slab), jnp.bfloat16)
    vmem = pl.BlockSpec(memory_space=pltpu.VMEM)
    hbm = pl.BlockSpec(memory_space=pl.ANY)
    dma = pltpu.SemaphoreType.DMA
    outs = pl.pallas_call(
        functools.partial(kernel, sizes),
        out_shape=(block, block, jax.ShapeDtypeStruct((n_params, 1, slab), jnp.float32), block),
        in_specs=[pl.BlockSpec(memory_space=pltpu.SMEM)]
        + [hbm] * 5
        + [vmem] * 4,
        out_specs=(hbm, hbm, vmem, hbm),
        scratch_shapes=[
            pltpu.VMEM((rows, slab), jnp.bfloat16),
            pltpu.VMEM((rows, slab), jnp.bfloat16),
            pltpu.VMEM((rows, slab), jnp.bfloat16),
            pltpu.VMEM((rows, slab), jnp.bfloat16),
            pltpu.VMEM((rows, slab), jnp.bfloat16),
            pltpu.VMEM(filters.shape[1:], jnp.bfloat16),
            pltpu.VMEM((n_seq, rows, slab), jnp.bfloat16),
            pltpu.VMEM((n_seq, rows, slab), jnp.bfloat16),
            pltpu.VMEM((n_seq + 1, 2 * rows, slab), jnp.bfloat16),
            pltpu.VMEM((rows, slab), jnp.float32),
            pltpu.VMEM((n_seq, rows, 128), jnp.float32),
            pltpu.VMEM((rows, 128), jnp.float32),
            pltpu.VMEM((rows, 128), jnp.float32),
            pltpu.VMEM((n_chan, 8, rows), jnp.float32),
            pltpu.VMEM((n_seq, 8, rows), jnp.float32),
            pltpu.VMEM((n_chan, 8, rows), jnp.float32),
            pltpu.VMEM((n_seq, 8, slab), jnp.float32),
            dma((chunks,)),
            dma((4,)),
            dma((2,)),
            dma((2, n_seq, chunks)),
            dma((2, n_seq, chunks)),
            dma((2, n_chan)),
            dma((2, n_seq)),
            dma((2, n_chan)),
            dma((2, n_seq)),
            dma((2, chunks)),
        ],
        compiler_params=pltpu.CompilerParams(
            collective_id=0, has_side_effects=True, vmem_limit_bytes=60 * 2**20
        ),
    )(
        order,
        fwd_in[0],
        saved_in[0],
        saved_conv[0],
        grad_out[0],
        filters[0],
        mix_params.transpose(1, 0, 2),
        *transform_tables(rows),
    )
    layer_out, input_grad, param_grad, received = store(*outs)
    return (layer_out[None], input_grad[None], param_grad.transpose(1, 0, 2), received[None])


def solution(mesh):
    spread = P("pipe", "seq", "chan")
    shared = P("pipe", None, "chan")
    return jax.shard_map(
        functools.partial(per_device, mesh.shape["seq"], mesh.shape["chan"]),
        mesh=mesh,
        in_specs=(spread, spread, spread, spread, shared, shared, P()),
        out_specs=(spread, spread, shared, spread),
        check_vma=False,
    )
```

```python
import functools

import jax
import jax.numpy as jnp
import numpy as np
from jax import lax
from jax.experimental import pallas as pl
from jax.experimental.pallas import tpu as pltpu
from jax.sharding import PartitionSpec as P

EPSILON = 1e-05
MESH = pl.DeviceIdType.MESH


def transform_tables(rows):
    period = 2 * rows
    angle = (
        2.0 * np.pi / period * (np.arange(rows)[:, None] + 0.5) * np.arange(period)[None, :]
    )
    forward = np.concatenate([np.cos(angle), -np.sin(angle)], axis=0)
    inverse = (forward[:, rows:] / rows).T
    enter = np.stack([forward[:, :rows], inverse.T])
    leave = np.stack([inverse, forward[:, :rows].T])
    return tuple(jnp.asarray(t, jnp.bfloat16) for t in (forward, enter, leave))


def fold_lanes(values):
    lanes = 128
    total = values[:, :lanes]
    for at in range(lanes, values.shape[1], lanes):
        total = total + values[:, at : at + lanes]
    return total


def widen(column, width):
    return jnp.concatenate([column] * (width // column.shape[1]), axis=1)


def kernel(
    sizes,
    order,
    fwd_in,
    saved_in_hbm,
    saved_conv_hbm,
    grad_out_hbm,
    filters_hbm,
    params,
    forward_tab,
    enter_tab,
    leave_tab,
    layer_out_hbm,
    input_grad_hbm,
    param_grad,
    received,
    layer_out,
    input_grad,
    saved_in,
    saved_conv,
    grad_out,
    filters,
    own_all,
    grad_all,
    spectra,
    grad_normed,
    column_all,
    saved_column,
    cross_lanes,
    square_rows,
    rms_rows,
    cross_rows,
    sum_rows,
    load_sem,
    operand_sem,
    result_sem,
    send_sem,
    recv_sem,
    square_sem,
    rms_sem,
    cross_sem,
    sum_sem,
    relay_sem,
):
    n_seq, n_chan, channels, chunks = sizes
    rows, slab = saved_in.shape
    width = slab // chunks
    chips = n_seq // 2
    me = lax.axis_index("seq")
    my_chan = lax.axis_index("chan")
    pipe = lax.axis_index("pipe")
    chip, core = me // 2, me % 2
    sibling = chip * 2 + 1 - core

    def columns(c):
        if isinstance(c, int):
            return pl.ds(c * width, width)
        return pl.ds(pl.multiple_of(c * width, width), width)

    def same_core(j):
        return lax.rem(chip + j, chips) * 2 + core

    def other_core(j):
        return lax.rem(chip + j, chips) * 2 + 1 - core

    def block_copy(kind, slot, c, k, target):
        buffer = own_all if kind == 0 else grad_all
        return pltpu.make_async_remote_copy(
            src_ref=buffer.at[slot, :, columns(c)],
            dst_ref=buffer.at[slot, :, columns(c)],
            send_sem=send_sem.at[kind, k, c],
            recv_sem=recv_sem.at[kind, slot, c],
            device_id={"seq": target},
            device_id_type=MESH,
        )

    def own_copies(kind, c):
        found = [block_copy(kind, me, c, j, same_core(j)) for j in range(1, chips)]
        return found + [block_copy(kind, me, c, 0, sibling)]

    def relay_copies(kind, c):
        return [
            block_copy(kind, same_core(j), c, chips - 1 + j, sibling) for j in range(1, chips)
        ]

    def start_own(kind, c):
        for copy in own_copies(kind, c):
            copy.start()

    def relay(kind, c):
        for j, copy in enumerate(relay_copies(kind, c)):
            block_copy(kind, same_core(j + 1), c, 0, sibling).wait_recv()
            copy.start()

    def arrive(kind, slot, c):
        block_copy(kind, slot, c, 0, sibling).wait_recv()

    def small_copies(buffer, sems, axis, index, count):
        return [
            pltpu.make_async_remote_copy(
                src_ref=buffer.at[index],
                dst_ref=buffer.at[index],
                send_sem=sems.at[0, j],
                recv_sem=sems.at[1, index],
                device_id={axis: lax.rem(index + j, count)},
                device_id_type=MESH,
            )
            for j in range(1, count)
        ]

    def small_wait(buffer, sems, axis, index, count):
        for j in range(1, count):
            peer = lax.rem(index + j, count)
            pltpu.make_async_remote_copy(
                src_ref=buffer.at[peer],
                dst_ref=buffer.at[peer],
                send_sem=sems.at[0, j],
                recv_sem=sems.at[1, peer],
                device_id={axis: peer},
                device_id_type=MESH,
            ).wait_recv()

    def partner_copy(source, c):
        return pltpu.make_async_remote_copy(
            src_ref=source.at[:, columns(c)],
            dst_ref=received.at[:, columns(c)],
            send_sem=relay_sem.at[0, c],
            recv_sem=relay_sem.at[1, c],
            device_id={"pipe": 1 - pipe},
            device_id_type=MESH,
        )

    def load_copy(c):
        return pltpu.make_async_copy(
            fwd_in.at[:, columns(c)], own_all.at[me, :, columns(c)], load_sem.at[c]
        )

    operands = [
        pltpu.make_async_copy(source, target, operand_sem.at[i])
        for i, (source, target) in enumerate(
            (
                (saved_in_hbm, saved_in),
                (filters_hbm, filters),
                (grad_out_hbm, grad_out),
                (saved_conv_hbm, saved_conv),
            )
        )
    ]
    for c in range(chunks):
        load_copy(c).start()
    for copy in operands:
        copy.start()

    barrier = pltpu.get_barrier_semaphore()
    for j in range(1, n_seq):
        pl.semaphore_signal(
            barrier, inc=1, device_id={"seq": lax.rem(me + j, n_seq)}, device_id_type=MESH
        )
    for j in range(1, n_chan):
        pl.semaphore_signal(
            barrier, inc=1, device_id={"chan": lax.rem(my_chan + j, n_chan)}, device_id_type=MESH
        )
    pl.semaphore_signal(barrier, inc=1, device_id={"pipe": 1 - pipe}, device_id_type=MESH)
    pl.semaphore_wait(barrier, n_seq + n_chan - 1)

    early = chunks // 4
    middle = chunks // 2
    for c in range(chunks):
        load_copy(c).wait()
        if c < early:
            start_own(0, c)

    def squares(read):
        def step(c, total):
            part = read(c).astype(jnp.float32)
            return total + fold_lanes(part * part)

        lanes = lax.fori_loop(0, chunks, step, jnp.zeros((rows, 128), jnp.float32))
        return jnp.sum(lanes.T, axis=0, keepdims=True)

    fwd_row = squares(lambda c: own_all[me, :, columns(c)])
    operands[0].wait()
    saved_row = squares(lambda c: saved_in[:, columns(c)])
    square_rows[my_chan] = jnp.concatenate([fwd_row, saved_row] * 4, axis=0)
    for copy in small_copies(square_rows, square_sem, "chan", my_chan, n_chan):
        copy.start()

    def filter_step(c, carry):
        cols = columns(c)
        spectra[0, :, cols] = jnp.zeros((2 * rows, width), jnp.bfloat16)
        spectra[1, :, cols] = jnp.dot(
            forward_tab[:, rows:], filters[:rows, cols], preferred_element_type=jnp.float32
        ).astype(jnp.bfloat16)

        def window(d, inner):
            taps = filters[pl.ds(pl.multiple_of((d - 1) * rows, rows), 2 * rows), cols]
            spectra[d + 1, :, cols] = jnp.dot(
                forward_tab[...], taps, preferred_element_type=jnp.float32
            ).astype(jnp.bfloat16)
            return inner

        return lax.fori_loop(1, n_seq, window, carry)

    operands[1].wait()
    lax.fori_loop(0, middle, filter_step, 0)

    small_wait(square_rows, square_sem, "chan", my_chan, n_chan)
    total_squares = square_rows[0]
    for j in range(1, n_chan):
        total_squares = total_squares + square_rows[j]
    inv_rows = lax.rsqrt(total_squares / channels + EPSILON)
    rms_rows[me] = inv_rows
    for copy in small_copies(rms_rows, rms_sem, "seq", me, n_seq):
        copy.start()
    saved_column[...] = jnp.broadcast_to(inv_rows[1:2], (rows, rows)).T

    def param(index, cols):
        return params[index, :, cols]

    def grad_conv_step(c, carry):
        cols = columns(c)
        scaled = (
            saved_in[:, cols].astype(jnp.float32) * widen(saved_column[...], width) * param(0, cols)
        )
        query = scaled * param(1, cols) + param(2, cols)
        grad_all[me, :, cols] = (grad_out[:, cols].astype(jnp.float32) * query).astype(jnp.bfloat16)
        start_own(1, c)
        return carry

    operands[2].wait()
    lax.fori_loop(0, chunks, grad_conv_step, 0)
    lax.fori_loop(middle, chunks, filter_step, 0)
    operands[3].wait()

    small_wait(rms_rows, rms_sem, "seq", me, n_seq)
    for s in range(n_seq):
        column_all[s] = jnp.broadcast_to(rms_rows[s, 0:1], (rows, rows)).T

    my_position = order[me]

    def long_conv(kind, c, signal):
        cols = columns(c)

        def term(slot, sums):
            distance = my_position - order[slot] if kind == 0 else order[slot] - my_position
            entering = jnp.dot(
                enter_tab[kind], signal(slot), preferred_element_type=jnp.float32
            )
            window = spectra[jnp.maximum(distance, -1) + 1, :, cols].astype(jnp.float32)
            data_real, data_imag = entering[:rows], entering[rows:]
            tap_real, tap_imag = window[:rows], window[rows:]
            if kind == 0:
                real = tap_real * data_real - tap_imag * data_imag
                imag = tap_real * data_imag + tap_imag * data_real
            else:
                real = tap_real * data_real + tap_imag * data_imag
                imag = tap_real * data_imag - tap_imag * data_real
            if sums is None:
                return real, imag
            return sums[0] + real, sums[1] + imag

        sums = term(me, None)
        arrive(kind, sibling, c)
        sums = term(sibling, sums)
        for j in range(1, chips):
            sums = term(same_core(j), sums)
        for j in range(1, chips):
            arrive(kind, other_core(j), c)
            sums = term(other_core(j), sums)
        spectrum = jnp.concatenate(sums, axis=0).astype(jnp.bfloat16)
        return jnp.dot(leave_tab[kind], spectrum, preferred_element_type=jnp.float32).astype(
            jnp.bfloat16
        )

    def backward_step(c, carry):
        cols = columns(c)
        relay(1, c)
        grad_mixed = long_conv(1, c, lambda slot: grad_all[slot, :, cols]).astype(jnp.float32)
        normed = saved_in[:, cols].astype(jnp.float32) * widen(saved_column[...], width)
        scaled = normed * param(0, cols)
        key = scaled * param(3, cols) + param(4, cols)
        value = scaled * param(5, cols) + param(6, cols)
        grad_query = grad_out[:, cols].astype(jnp.float32) * saved_conv[:, cols].astype(jnp.float32)
        grad_key = grad_mixed * value
        grad_value = grad_mixed * key
        grad_scaled = (
            grad_query * param(1, cols) + grad_key * param(3, cols) + grad_value * param(5, cols)
        )
        terms = [
            grad_scaled * normed,
            grad_query * scaled,
            grad_query,
            grad_key * scaled,
            grad_key,
            grad_value * scaled,
            grad_value,
        ]
        sums = [jnp.sum(term, axis=0, keepdims=True) for term in terms]
        sum_rows[me, :, cols] = jnp.concatenate(sums + sums[:1], axis=0)
        outer = grad_scaled * param(0, cols)
        grad_normed[:, cols] = outer
        cross_lanes[...] += fold_lanes(outer * normed)
        return carry

    cross_lanes[...] = jnp.zeros_like(cross_lanes)
    for c in range(early):
        relay(0, c)
    lax.fori_loop(0, chunks - 2, backward_step, 0)
    for c in range(early, middle):
        start_own(0, c)
    backward_step(chunks - 2, 0)
    for c in range(middle, chunks):
        start_own(0, c)
    backward_step(chunks - 1, 0)

    cross_rows[my_chan] = jnp.broadcast_to(
        jnp.sum(cross_lanes[...].T, axis=0, keepdims=True), (8, rows)
    )
    for copy in small_copies(cross_rows, cross_sem, "chan", my_chan, n_chan):
        copy.start()
    for copy in small_copies(sum_rows, sum_sem, "seq", me, n_seq):
        copy.start()

    def forward_step(c, carry):
        cols = columns(c)

        def mixed(slot):
            scaled = (
                own_all[slot, :, cols].astype(jnp.float32)
                * widen(column_all[slot], width)
                * param(0, cols)
            )
            key = scaled * param(3, cols) + param(4, cols)
            value = scaled * param(5, cols) + param(6, cols)
            return (key * value).astype(jnp.bfloat16)

        conv = long_conv(0, c, mixed).astype(jnp.float32)
        inputs = own_all[me, :, cols].astype(jnp.float32)
        scaled = inputs * widen(column_all[me], width) * param(0, cols)
        query = scaled * param(1, cols) + param(2, cols)
        layer_out[:, cols] = (inputs + query * conv).astype(jnp.bfloat16)

        @pl.when(pipe == 0)
        def _():
            partner_copy(layer_out, c).start()

        return carry

    lax.fori_loop(0, early, forward_step, 0)

    small_wait(cross_rows, cross_sem, "chan", my_chan, n_chan)
    cross = cross_rows[0]
    for j in range(1, n_chan):
        cross = cross + cross_rows[j]
    cross_lanes[...] = jnp.broadcast_to(cross[0:1] / channels, (rows, rows)).T

    def input_grad_step(c, carry):
        cols = columns(c)
        inverse = widen(saved_column[...], width)
        normed = saved_in[:, cols].astype(jnp.float32) * inverse
        inner = grad_normed[:, cols] - normed * widen(cross_lanes[...], width)
        input_grad[:, cols] = (
            grad_out[:, cols].astype(jnp.float32) + inverse * inner
        ).astype(jnp.bfloat16)

        @pl.when(pipe == 1)
        def _():
            partner_copy(input_grad, c).start()

        return carry

    lax.fori_loop(0, chunks, input_grad_step, 0)
    stores = [
        pltpu.make_async_copy(input_grad, input_grad_hbm, result_sem.at[0]),
        pltpu.make_async_copy(layer_out, layer_out_hbm, result_sem.at[1]),
    ]
    stores[0].start()

    def late_forward_step(c, carry):
        @pl.when(c + 1 < chunks)
        def _():
            relay(0, c + 1)

        return forward_step(c, carry)

    relay(0, early)
    lax.fori_loop(early, chunks, late_forward_step, 0)
    stores[1].start()

    small_wait(sum_rows, sum_sem, "seq", me, n_seq)
    total = sum_rows[0]
    for s in range(1, n_seq):
        total = total + sum_rows[s]
    for i in range(param_grad.shape[0]):
        param_grad[i] = total[i : i + 1]

    for c in range(chunks):
        for kind in range(2):
            for copy in own_copies(kind, c) + relay_copies(kind, c):
                copy.wait_send()
    for buffer, sems, axis, index, count in (
        (square_rows, square_sem, "chan", my_chan, n_chan),
        (cross_rows, cross_sem, "chan", my_chan, n_chan),
        (rms_rows, rms_sem, "seq", me, n_seq),
        (sum_rows, sum_sem, "seq", me, n_seq),
    ):
        for copy in small_copies(buffer, sems, axis, index, count):
            copy.wait_send()
    for c in range(chunks):
        partner_copy(layer_out, c).wait()
    for copy in stores:
        copy.wait()


def store_kernel(count, *refs):
    sources, targets, held = (refs[at * count : (at + 1) * count] for at in range(3))
    sems = refs[3 * count]
    fetches = [pltpu.make_async_copy(sources[i], held[i], sems.at[0, i]) for i in range(count)]
    stores = [pltpu.make_async_copy(held[i], targets[i], sems.at[1, i]) for i in range(count)]
    for copy in fetches:
        copy.start()
    for fetch, copy in zip(fetches, stores):
        fetch.wait()
        copy.start()
    for copy in stores:
        copy.wait()


def store(*arrays):
    count = len(arrays)
    anywhere = pl.BlockSpec(memory_space=pl.ANY)
    return pl.pallas_call(
        functools.partial(store_kernel, count),
        out_shape=tuple(jax.ShapeDtypeStruct(a.shape, a.dtype) for a in arrays),
        in_specs=[anywhere] * count,
        out_specs=(anywhere,) * count,
        scratch_shapes=[pltpu.VMEM(a.shape, a.dtype) for a in arrays]
        + [pltpu.SemaphoreType.DMA((2, count))],
    )(*arrays)


def per_device(n_seq, n_chan, fwd_in, saved_in, saved_conv, grad_out, filters, mix_params, order):
    rows, slab = fwd_in.shape[1:]
    chunks = 8
    sizes = (n_seq, n_chan, slab * n_chan, chunks)
    n_params = mix_params.shape[1]
    block = jax.ShapeDtypeStruct((rows, slab), jnp.bfloat16)
    vmem = pl.BlockSpec(memory_space=pltpu.VMEM)
    hbm = pl.BlockSpec(memory_space=pl.ANY)
    dma = pltpu.SemaphoreType.DMA
    outs = pl.pallas_call(
        functools.partial(kernel, sizes),
        out_shape=(block, block, jax.ShapeDtypeStruct((n_params, 1, slab), jnp.float32), block),
        in_specs=[pl.BlockSpec(memory_space=pltpu.SMEM)]
        + [hbm] * 5
        + [vmem] * 4,
        out_specs=(hbm, hbm, vmem, hbm),
        scratch_shapes=[
            pltpu.VMEM((rows, slab), jnp.bfloat16),
            pltpu.VMEM((rows, slab), jnp.bfloat16),
            pltpu.VMEM((rows, slab), jnp.bfloat16),
            pltpu.VMEM((rows, slab), jnp.bfloat16),
            pltpu.VMEM((rows, slab), jnp.bfloat16),
            pltpu.VMEM(filters.shape[1:], jnp.bfloat16),
            pltpu.VMEM((n_seq, rows, slab), jnp.bfloat16),
            pltpu.VMEM((n_seq, rows, slab), jnp.bfloat16),
            pltpu.VMEM((n_seq + 1, 2 * rows, slab), jnp.bfloat16),
            pltpu.VMEM((rows, slab), jnp.float32),
            pltpu.VMEM((n_seq, rows, 128), jnp.float32),
            pltpu.VMEM((rows, 128), jnp.float32),
            pltpu.VMEM((rows, 128), jnp.float32),
            pltpu.VMEM((n_chan, 8, rows), jnp.float32),
            pltpu.VMEM((n_seq, 8, rows), jnp.float32),
            pltpu.VMEM((n_chan, 8, rows), jnp.float32),
            pltpu.VMEM((n_seq, 8, slab), jnp.float32),
            dma((chunks,)),
            dma((4,)),
            dma((2,)),
            dma((2, n_seq, chunks)),
            dma((2, n_seq, chunks)),
            dma((2, n_chan)),
            dma((2, n_seq)),
            dma((2, n_chan)),
            dma((2, n_seq)),
            dma((2, chunks)),
        ],
        compiler_params=pltpu.CompilerParams(
            collective_id=0, has_side_effects=True, vmem_limit_bytes=60 * 2**20
        ),
    )(
        order,
        fwd_in[0],
        saved_in[0],
        saved_conv[0],
        grad_out[0],
        filters[0],
        mix_params.transpose(1, 0, 2),
        *transform_tables(rows),
    )
    layer_out, input_grad, param_grad, received = store(*outs)
    return (layer_out[None], input_grad[None], param_grad.transpose(1, 0, 2), received[None])


def solution(mesh):
    spread = P("pipe", "seq", "chan")
    shared = P("pipe", None, "chan")
    return jax.shard_map(
        functools.partial(per_device, mesh.shape["seq"], mesh.shape["chan"]),
        mesh=mesh,
        in_specs=(spread, spread, spread, spread, shared, shared, P()),
        out_specs=(spread, spread, shared, spread),
        check_vma=False,
    )
```
